32 devices in a mesh: groups: 2 (over y), dp: 4 (over z), tensor: 4 (over x, core).
Axes of the slice: x: 2, y: 2, z: 4, core: 2. Of those that a mesh axis runs over, the one named last changes fastest.
Arguments:
- hidden_acts: bfloat16 [1024, 28672], P(('groups', 'dp'), 'tensor'), parts along dimension 0, may hold values from -40 to 40
- out_grads: bfloat16 [1024, 8192], P(('groups', 'dp'), 'tensor'), parts along dimension 0, may hold values from -40 to 40
- proj_in: bfloat16 [28672, 64], P('tensor'), may hold values from -0.03125 to 0.03125
- proj_out: bfloat16 [8192, 64], P('tensor'), may hold values from -0.0625 to 0.0625
- query_sketches: bfloat16 [64, 4096], P('dp'), may hold values from -0.09375 to 0.09375
Outputs:
- scores: float32 [2, 64], P('groups', 'dp'), parts along dimension 0
The draws below stay inside these ranges and needn't reach their ends.
There are 2 independent parts, one for each index of `groups`. The reference program is written for one: setup_inputs(seed, part) draws one part's arguments, and reference() takes and returns one part's arrays. A program takes and returns all parts, laid end to end along the dimension named above; an argument that names none is the same for every part. Nothing has to cross between parts.
All inputs are finite; a program needn't handle non-finite values.
Results may differ from the reference program's by a relative error of at most 0.0032.
Values sent between devices are 32-bit elements; how exact they have to be, the bound alone decides.
A program may use at most 64 MiB of HBM per device.

```python
import math
import jax
import jax.numpy as jnp
from jax import lax

D = 8192
FF = 28672
RANK = 64
LEN = 512
TOKENS = 512
EXAMPLES = 1
QUERIES = 64


def rough_rows(key, rows, cols, rise, top):
    keys = jax.random.split(key, 3)
    base = jax.random.normal(keys[0], (rows, cols), jnp.float32)
    row_scale = jnp.exp(jax.random.uniform(keys[1], (rows, 1), jnp.float32) * math.log(top)) / math.sqrt(top)
    col_scale = jnp.exp((jax.random.uniform(keys[2], (1, cols), jnp.float32) - 0.5) * math.log(10.0))
    position = jnp.arange(rows, dtype=jnp.float32).reshape(rows, 1) / rows
    growth = jnp.exp(position * math.log(rise)) / math.sqrt(rise)
    return jnp.clip(base * row_scale * col_scale * growth, -40.0, 40.0)


def draw_hidden_acts(key, part):
    key = jax.random.fold_in(key, 11)
    values = rough_rows(key, TOKENS, FF, 3.0, 10.0)
    return values.astype(jnp.bfloat16)


def draw_out_grads(key, part):
    key = jax.random.fold_in(key, 23)
    values = rough_rows(key, TOKENS, D, 3.0, 10.0)
    return values.astype(jnp.bfloat16)


def levels(own_key, extent, shards, smallest, high):
    def one(dim, parts):
        heights = jax.random.uniform(jax.random.fold_in(jax.random.fold_in(own_key, 6), dim), (parts,), jnp.float32, smallest / len(shards), high / len(shards))
        return jnp.repeat(jnp.exp(heights), extent[dim] // parts).reshape((-1,) + (1,) * (len(extent) - dim - 1))

    gain = one(*shards[0])
    for cut in shards[1:]:
        gain = gain * one(*cut)
    return gain


def normal_values(stream_key, extent, deviation, most, pieces=(), kind=jnp.bfloat16):
    drawn = deviation * jax.random.normal(stream_key, extent, jnp.float32)
    if pieces:
        drawn = drawn * levels(stream_key, extent, pieces, -0.22, 0.18)
    return jnp.clip(drawn, -most, most).astype(kind)


def setup_inputs(seed: int = 0, part: int = 0) -> dict:
    arg_keys = jax.random.split(jax.random.key(seed), 6)
    part_splits = jax.random.split(jax.random.fold_in(arg_keys[5], part), 6)
    return {
        "hidden_acts": draw_hidden_acts(jax.random.fold_in(jax.random.fold_in(arg_keys[5], part), 71), part),
        "out_grads": draw_out_grads(jax.random.fold_in(jax.random.fold_in(arg_keys[5], part), 71), part),
        "proj_in": normal_values(arg_keys[2], (FF, RANK), FF ** -0.5, 0.03125, ((0, 4),)),
        "proj_out": normal_values(arg_keys[3], (D, RANK), D ** -0.5, 0.0625, ((0, 4),)),
        "query_sketches": normal_values(arg_keys[4], (QUERIES, RANK * RANK), (RANK * RANK) ** -0.5, 0.09375, ((0, 4),)),
    }


def inverse_of(cov):
    size = cov.shape[0]
    eye = jnp.eye(size, dtype=jnp.float32)
    damped = cov + 0.1 * jnp.trace(cov) / size * eye
    factor = jnp.linalg.cholesky(damped)
    return jax.scipy.linalg.cho_solve((factor, True), eye)

def reference(hidden_acts, out_grads, proj_in, proj_out, query_sketches):
    highest = lax.Precision.HIGHEST
    in_side = jnp.dot(hidden_acts.astype(jnp.float32), proj_in.astype(jnp.float32), preferred_element_type=jnp.float32)
    out_side = jnp.dot(out_grads.astype(jnp.float32), proj_out.astype(jnp.float32), preferred_element_type=jnp.float32)
    in_cov = jnp.dot(in_side.T, in_side, precision=highest) / TOKENS
    out_cov = jnp.dot(out_side.T, out_side, precision=highest) / TOKENS
    in_inv = inverse_of(in_cov)
    out_inv = inverse_of(out_cov)
    in_rows = in_side.reshape(EXAMPLES, LEN, RANK)
    out_rows = out_side.reshape(EXAMPLES, LEN, RANK)
    sketch = jnp.einsum('etr,ets->ers', in_rows, out_rows, precision=highest)
    precond = jnp.einsum('ar,ers,sb->eab', in_inv, sketch, out_inv, precision=highest)
    factor = 1.0 / math.sqrt(LEN)
    precond = (precond * factor).reshape(EXAMPLES, RANK * RANK).astype(jnp.bfloat16)
    return jnp.dot(precond.astype(jnp.float32), query_sketches.T.astype(jnp.float32), preferred_element_type=jnp.float32)
```

```python
import functools
import math

import jax
import jax.numpy as jnp
from jax import lax
from jax.experimental import pallas as pl
from jax.experimental.pallas import tpu as pltpu
from jax.sharding import PartitionSpec as P

MESH = pl.DeviceIdType.MESH
HIGHEST = lax.Precision.HIGHEST
IN_CHUNKS = 4
BLOCK = 4


def repeat(start, stop, body):
    if stop - start <= 8:
        for k in range(start, stop):
            body(k)
    else:
        lax.fori_loop(start, stop, lambda k, c: (body(k), c)[1], 0)


def negated_inverses(both, width):
    shape = both.shape
    row = lax.broadcasted_iota(jnp.int32, shape, 0)
    lane = lax.broadcasted_iota(jnp.int32, shape, 1)
    col = lane % width
    side = lane - col
    lane1 = lax.broadcasted_iota(jnp.int32, (1, shape[1]), 1)
    col1 = lane1 % width
    m = both
    for k0 in range(0, width, BLOCK):
        js = range(BLOCK)
        cols = [jnp.take_along_axis(m, side + (k0 + j), axis=1) for j in js]
        d = [[cols[j][k0 + i : k0 + i + 1, :] for j in js] for i in js]
        in_block1 = (col1 >= k0) & (col1 < k0 + BLOCK)
        w = [
            jnp.where(in_block1, jnp.where(col1 == k0 + i, -1.0, 0.0), m[k0 + i : k0 + i + 1, :])
            for i in js
        ]
        for p in js:
            r = 1.0 / d[p][p]
            w[p] = w[p] * r
            for j in range(p + 1, BLOCK):
                d[p][j] = d[p][j] * r
            for i in js:
                if i != p:
                    f = d[i][p]
                    w[i] = w[i] - f * w[p]
                    for j in range(p + 1, BLOCK):
                        d[i][j] = d[i][j] - f * d[p][j]
        in_rows = (row >= k0) & (row < k0 + BLOCK)
        in_cols = (col >= k0) & (col < k0 + BLOCK)
        m = jnp.where(in_rows | in_cols, 0.0, m)
        for j in js:
            c = jnp.where(in_rows, jnp.where(row == k0 + j, -1.0, 0.0), cols[j])
            m = m - c * w[j]
    return m


def kernel(
    n_t, n_dp, h_hbm, g_hbm, pi_hbm, po_hbm, q_hbm, out_ref,
    h_v, g_v, pi_v, po_v, q_v, part, landed, tokens, pay,
    load_sem, h_sem, a_send, a_recv, b_send, b_recv, c_send, c_recv,
):
    me_t = lax.axis_index("tensor")
    me_dp = lax.axis_index("dp")
    width = pi_v.shape[0]
    rows = part.shape[0]
    share = rows // n_t
    span = min(32, n_dp)
    seqs = n_dp // span
    token_count = rows * n_dp
    factor = 1.0 / math.sqrt(rows * span)

    step = h_v.shape[1] // IN_CHUNKS
    loads = [
        pltpu.make_async_copy(g_hbm, g_v, load_sem.at[0]),
        pltpu.make_async_copy(po_hbm, po_v, load_sem.at[1]),
    ]
    chunks = []
    for c in range(IN_CHUNKS):
        at = pl.ds(c * step, step)
        chunks.append(
            (
                pltpu.make_async_copy(h_hbm.at[:, at], h_v.at[:, at], h_sem.at[2 * c]),
                pltpu.make_async_copy(pi_hbm.at[:, at], pi_v.at[:, at], h_sem.at[2 * c + 1]),
            )
        )
    q_load = pltpu.make_async_copy(q_hbm, q_v, load_sem.at[2])
    for copy in loads:
        copy.start()
    for pair in chunks:
        for copy in pair:
            copy.start()
    q_load.start()

    barrier = pltpu.get_barrier_semaphore()

    def greet_t(k):
        pl.semaphore_signal(barrier, inc=1, device_id={"tensor": lax.rem(me_t + k, n_t)}, device_id_type=MESH)

    def greet_dp(k):
        pl.semaphore_signal(barrier, inc=1, device_id={"dp": lax.rem(me_dp + k, n_dp)}, device_id_type=MESH)

    repeat(1, n_t, greet_t)
    repeat(1, n_dp, greet_dp)

    nt = (((1,), (1,)), ((), ()))
    tn = (((0,), (0,)), ((), ()))
    for copy in loads:
        copy.wait()
    part[:, width:] = lax.dot_general(g_v[...], po_v[...], nt, preferred_element_type=jnp.float32)
    total = None
    for c, pair in enumerate(chunks):
        for copy in pair:
            copy.wait()
        at = pl.ds(c * step, step)
        term = lax.dot_general(h_v[:, at], pi_v[:, at], nt, preferred_element_type=jnp.float32)
        total = term if total is None else total + term
    part[:, :width] = total

    pl.semaphore_wait(barrier, (n_t - 1) + (n_dp - 1))

    def a_copy(k):
        peer = lax.rem(me_t + k, n_t)
        return pltpu.make_async_remote_copy(
            src_ref=part.at[pl.ds(pl.multiple_of(peer * share, share), share)],
            dst_ref=landed.at[k - 1],
            send_sem=a_send.at[k - 1],
            recv_sem=a_recv.at[k - 1],
            device_id={"tensor": peer},
            device_id_type=MESH,
        )

    a_copies = [a_copy(k) for k in range(1, n_t)]
    for copy in a_copies:
        copy.start()
    mine = part[pl.ds(pl.multiple_of(me_t * share, share), share), :]
    for k, copy in enumerate(a_copies):
        copy.wait_recv()
        mine = mine + landed[k]
    tokens[me_dp] = mine

    def b_copy(k, slot):
        return pltpu.make_async_remote_copy(
            src_ref=tokens.at[slot],
            dst_ref=tokens.at[slot],
            send_sem=b_send.at[k - 1],
            recv_sem=b_recv.at[k - 1],
            device_id={"dp": lax.rem(me_dp + k, n_dp)},
            device_id_type=MESH,
        )

    repeat(1, n_dp, lambda k: b_copy(k, me_dp).start())
    repeat(1, n_dp, lambda k: b_copy(k, lax.rem(me_dp + n_dp - k, n_dp)).wait_recv())

    upper = lax.broadcasted_iota(jnp.int32, (width, 2 * width), 1) >= width
    upper_half = lax.broadcasted_iota(jnp.int32, (width // 2, 2 * width), 1) >= width
    upper1 = lax.broadcasted_iota(jnp.int32, (1, 2 * width), 1) >= width
    half = width // 2
    covs = None
    for s in range(seqs):
        own = tokens[s * span : (s + 1) * span].reshape(span * share, 2 * width)
        gram = lax.dot_general(own, own, tn, precision=HIGHEST, preferred_element_type=jnp.float32)
        cov = jnp.where(upper, gram[width:], gram[:width])
        covs = cov if covs is None else covs + cov
        swapped = pltpu.roll(gram[half:width], width, 1)
        pay[me_t, pl.ds(width + s * half, half), :] = jnp.where(upper_half, gram[:half], swapped)
    pay[me_t, :width, :] = covs

    def c_copy(k, slot):
        return pltpu.make_async_remote_copy(
            src_ref=pay.at[slot],
            dst_ref=pay.at[slot],
            send_sem=c_send.at[k - 1],
            recv_sem=c_recv.at[k - 1],
            device_id={"tensor": lax.rem(me_t + k, n_t)},
            device_id_type=MESH,
        )

    for k in range(1, n_t):
        c_copy(k, me_t).start()
    for k in range(1, n_t):
        c_copy(k, lax.rem(me_t + n_t - k, n_t)).wait_recv()
    full = pay[0]
    for t in range(1, n_t):
        full = full + pay[t]

    both = full[:width] / token_count
    row = lax.broadcasted_iota(jnp.int32, both.shape, 0)
    col = lax.broadcasted_iota(jnp.int32, both.shape, 1) % width
    diag = jnp.sum(jnp.where(row == col, both, 0.0), axis=0, keepdims=True)
    trace_in = jnp.sum(jnp.where(upper1, 0.0, diag), axis=1, keepdims=True)
    trace_out = jnp.sum(jnp.where(upper1, diag, 0.0), axis=1, keepdims=True)
    damp = 0.1 * jnp.where(upper1, trace_out, trace_in) / width
    both = both + jnp.where(row == col, damp, 0.0)
    inverse = negated_inverses(both, width)
    in_inv = inverse[:, :width]
    out_inv = jnp.where(upper, inverse, pltpu.roll(inverse, width, 1))

    q_load.wait()
    for s in range(seqs):
        packed = full[width + s * half : width + (s + 1) * half]
        sketch = jnp.concatenate([pltpu.roll(packed, width, 1)[:, :width], packed[:, :width]], axis=0)
        left = jnp.dot(in_inv, sketch, precision=HIGHEST, preferred_element_type=jnp.float32)
        precond = jnp.dot(left, out_inv, precision=HIGHEST, preferred_element_type=jnp.float32)
        precond = (precond * factor).astype(jnp.bfloat16).astype(jnp.float32)
        sums = [None] * 4
        for j in range(half):
            weights = jnp.where(upper1, precond[2 * j + 1 : 2 * j + 2, :], precond[2 * j : 2 * j + 1, :])
            term = q_v[:, 2 * width * j : 2 * width * (j + 1)].astype(jnp.float32) * weights
            sums[j % 4] = term if sums[j % 4] is None else sums[j % 4] + term
        acc = (sums[0] + sums[1]) + (sums[2] + sums[3])
        ones = jnp.ones((8, 2 * width), jnp.float32)
        scores = lax.dot_general(ones, acc, nt, precision=HIGHEST, preferred_element_type=jnp.float32)
        out_ref[s : s + 1, :] = scores[:1]

    for copy in a_copies:
        copy.wait_send()
    repeat(1, n_dp, lambda k: b_copy(k, me_dp).wait_send())
    for k in range(1, n_t):
        c_copy(k, me_t).wait_send()


def solution(mesh):
    n_t, n_dp = mesh.shape["tensor"], mesh.shape["dp"]

    def shards(hidden_acts, out_grads, proj_in, proj_out, query_sketches):
        rows, depth = hidden_acts.shape
        model = out_grads.shape[1]
        width = proj_in.shape[1]
        queries, flat = query_sketches.shape
        seqs = n_dp // min(32, n_dp)
        share = rows // n_t
        dma = pltpu.SemaphoreType.DMA
        f32, bf16 = jnp.float32, jnp.bfloat16
        return pl.pallas_call(
            functools.partial(kernel, n_t, n_dp),
            out_shape=jax.ShapeDtypeStruct((seqs, queries), f32),
            in_specs=[pl.BlockSpec(memory_space=pl.ANY)] * 5,
            out_specs=pl.BlockSpec(memory_space=pltpu.VMEM),
            scratch_shapes=[
                pltpu.VMEM((rows, depth), bf16),
                pltpu.VMEM((rows, model), bf16),
                pltpu.VMEM((width, depth), bf16),
                pltpu.VMEM((width, model), bf16),
                pltpu.VMEM((queries, flat), bf16),
                pltpu.VMEM((rows, 2 * width), f32),
                pltpu.VMEM((n_t - 1, share, 2 * width), f32),
                pltpu.VMEM((n_dp, share, 2 * width), f32),
                pltpu.VMEM((n_t, width + seqs * (width // 2), 2 * width), f32),
                dma((3,)),
                dma((2 * IN_CHUNKS,)),
                dma((n_t - 1,)),
                dma((n_t - 1,)),
                dma((n_dp - 1,)),
                dma((n_dp - 1,)),
                dma((n_t - 1,)),
                dma((n_t - 1,)),
            ],
            compiler_params=pltpu.CompilerParams(
                collective_id=0, has_side_effects=True, vmem_limit_bytes=48 * 1024 * 1024
            ),
        )(hidden_acts, out_grads, proj_in.T, proj_out.T, query_sketches)

    return jax.shard_map(
        shards,
        mesh=mesh,
        in_specs=(
            P(("groups", "dp"), "tensor"),
            P(("groups", "dp"), "tensor"),
            P("tensor", None),
            P("tensor", None),
            P("dp", None),
        ),
        out_specs=P("groups", "dp"),
        check_vma=False,
    )
```

```python
import functools
import math

import jax
import jax.numpy as jnp
from jax import lax
from jax.experimental import pallas as pl
from jax.experimental.pallas import tpu as pltpu
from jax.sharding import PartitionSpec as P

MESH = pl.DeviceIdType.MESH
HIGHEST = lax.Precision.HIGHEST
IN_CHUNKS = 4
BLOCK = 8


def repeat(start, stop, body):
    if stop - start <= 8:
        for k in range(start, stop):
            body(k)
    else:
        lax.fori_loop(start, stop, lambda k, c: (body(k), c)[1], 0)


def pair_of(n_t):
    return 2 if n_t % 2 == 0 else 1


def negated_inverses(both, width):
    shape = both.shape
    row = lax.broadcasted_iota(jnp.int32, shape, 0)
    lane = lax.broadcasted_iota(jnp.int32, shape, 1)
    col = lane % width
    side = lane - col
    lane1 = lax.broadcasted_iota(jnp.int32, (1, shape[1]), 1)
    col1 = lane1 % width
    m = both
    for k0 in range(0, width, BLOCK):
        js = range(BLOCK)
        cols = [jnp.take_along_axis(m, side + (k0 + j), axis=1) for j in js]
        d = [[cols[j][k0 + i : k0 + i + 1, :] for j in js] for i in js]
        in_block1 = (col1 >= k0) & (col1 < k0 + BLOCK)
        w = [
            jnp.where(in_block1, jnp.where(col1 == k0 + i, -1.0, 0.0), m[k0 + i : k0 + i + 1, :])
            for i in js
        ]
        for p in js:
            r = 1.0 / d[p][p]
            w[p] = w[p] * r
            for j in range(p + 1, BLOCK):
                d[p][j] = d[p][j] * r
            for i in js:
                if i != p:
                    f = d[i][p]
                    w[i] = w[i] - f * w[p]
                    for j in range(p + 1, BLOCK):
                        d[i][j] = d[i][j] - f * d[p][j]
        in_rows = (row >= k0) & (row < k0 + BLOCK)
        in_cols = (col >= k0) & (col < k0 + BLOCK)
        m = jnp.where(in_rows | in_cols, 0.0, m)
        for j in js:
            c = jnp.where(in_rows, jnp.where(row == k0 + j, -1.0, 0.0), cols[j])
            m = m - c * w[j]
    return m


def kernel(
    n_t, n_dp, h_hbm, g_hbm, pi_hbm, po_hbm, q_hbm, out_ref,
    h_v, g_v, pi_v, po_v, q_v, part, landed, tokens,
    load_sem, h_sem, a_send, a_recv, b_send, b_recv, c_send, c_recv,
):
    me_t = lax.axis_index("tensor")
    me_dp = lax.axis_index("dp")
    pair = pair_of(n_t)
    groups = n_t // pair
    other = me_t + 1 - 2 * lax.rem(me_t, 2)
    width = pi_v.shape[0]
    rows = part.shape[0]
    share = rows // n_t
    span = min(32, n_dp)
    seqs = n_dp // span
    token_count = rows * n_dp
    factor = 1.0 / math.sqrt(rows * span)

    step = h_v.shape[1] // IN_CHUNKS
    loads = [
        pltpu.make_async_copy(g_hbm, g_v, load_sem.at[0]),
        pltpu.make_async_copy(po_hbm, po_v, load_sem.at[1]),
    ]
    chunks = []
    for c in range(IN_CHUNKS):
        at = pl.ds(c * step, step)
        chunks.append(
            (
                pltpu.make_async_copy(h_hbm.at[:, at], h_v.at[:, at], h_sem.at[2 * c]),
                pltpu.make_async_copy(pi_hbm.at[:, at], pi_v.at[:, at], h_sem.at[2 * c + 1]),
            )
        )
    q_load = pltpu.make_async_copy(q_hbm, q_v, load_sem.at[2])
    for copy in loads:
        copy.start()
    for copies in chunks:
        for copy in copies:
            copy.start()
    q_load.start()

    barrier = pltpu.get_barrier_semaphore()

    def greet_t(k):
        pl.semaphore_signal(barrier, inc=1, device_id={"tensor": lax.rem(me_t + k, n_t)}, device_id_type=MESH)

    def greet_dp(k):
        for m in range(groups):
            peer = {"dp": lax.rem(me_dp + k, n_dp), "tensor": lax.rem(me_t + m * pair, n_t)}
            pl.semaphore_signal(barrier, inc=1, device_id=peer, device_id_type=MESH)

    repeat(1, n_t, greet_t)
    repeat(1, n_dp, greet_dp)

    nt = (((1,), (1,)), ((), ()))
    tn = (((0,), (0,)), ((), ()))
    for copy in loads:
        copy.wait()
    part[:, width:] = lax.dot_general(g_v[...], po_v[...], nt, preferred_element_type=jnp.float32)
    total = None
    for c, copies in enumerate(chunks):
        for copy in copies:
            copy.wait()
        at = pl.ds(c * step, step)
        term = lax.dot_general(h_v[:, at], pi_v[:, at], nt, preferred_element_type=jnp.float32)
        total = term if total is None else total + term
    part[:, :width] = total

    pl.semaphore_wait(barrier, (n_t - 1) + groups * (n_dp - 1))

    def a_copy(k):
        peer = lax.rem(me_t + k, n_t)
        return pltpu.make_async_remote_copy(
            src_ref=part.at[pl.ds(pl.multiple_of(peer * share, share), share)],
            dst_ref=landed.at[k - 1],
            send_sem=a_send.at[k - 1],
            recv_sem=a_recv.at[k - 1],
            device_id={"tensor": peer},
            device_id_type=MESH,
        )

    a_copies = [a_copy(k) for k in range(1, n_t)]
    for copy in a_copies:
        copy.start()
    mine = part[pl.ds(pl.multiple_of(me_t * share, share), share), :]
    for k, copy in enumerate(a_copies):
        copy.wait_recv()
        mine = mine + landed[k]
    my_slot = me_dp * n_t + me_t
    tokens[my_slot] = mine

    def slot_of(k, m):
        return lax.rem(me_dp + k, n_dp) * n_t + lax.rem(me_t + m * pair, n_t)

    def b_copy(k, m, slot):
        return pltpu.make_async_remote_copy(
            src_ref=tokens.at[slot],
            dst_ref=tokens.at[slot],
            send_sem=b_send.at[k, m],
            recv_sem=b_recv.at[k, m],
            device_id={"dp": lax.rem(me_dp + k, n_dp), "tensor": lax.rem(me_t + m * pair, n_t)},
            device_id_type=MESH,
        )

    def c_copy(k, m, slot):
        return pltpu.make_async_remote_copy(
            src_ref=tokens.at[slot],
            dst_ref=tokens.at[slot],
            send_sem=c_send.at[k, m],
            recv_sem=c_recv.at[k, m],
            device_id={"tensor": other},
            device_id_type=MESH,
        )

    def send(k):
        for m in range(groups):
            if not (isinstance(k, int) and k == 0 and m == 0):
                b_copy(k, m, my_slot).start()

    def take(k):
        for m in range(groups):
            slot = slot_of(n_dp - k, groups - m)
            if not (isinstance(k, int) and k == 0 and m == 0):
                b_copy(k, m, slot).wait_recv()
            if pair == 2:
                c_copy(k, m, slot).start()

    def other_of(slot):
        return slot + 1 - 2 * lax.rem(slot, 2)

    def take_other(k):
        for m in range(groups):
            slot = slot_of(n_dp - k, groups - m)
            c_copy(k, m, other_of(slot)).wait_recv()

    def sent(k):
        for m in range(groups):
            if not (isinstance(k, int) and k == 0 and m == 0):
                b_copy(k, m, my_slot).wait_send()
            if pair == 2:
                c_copy(k, m, slot_of(n_dp - k, groups - m)).wait_send()

    send(0)
    repeat(1, n_dp, send)
    take(0)
    repeat(1, n_dp, take)
    if pair == 2:
        take_other(0)
        repeat(1, n_dp, take_other)

    upper = lax.broadcasted_iota(jnp.int32, (width, 2 * width), 1) >= width
    upper1 = lax.broadcasted_iota(jnp.int32, (1, 2 * width), 1) >= width
    half = width // 2
    both = None
    grams = []
    for s in range(seqs):
        own = tokens[s * span * n_t : (s + 1) * span * n_t].reshape(span * rows, 2 * width)
        gram = lax.dot_general(own, own, tn, precision=HIGHEST, preferred_element_type=jnp.float32)
        cov = jnp.where(upper, gram[width:], gram[:width])
        both = cov if both is None else both + cov
        grams.append(gram)
    both = both / token_count
    row = lax.broadcasted_iota(jnp.int32, both.shape, 0)
    col = lax.broadcasted_iota(jnp.int32, both.shape, 1) % width
    diag = jnp.sum(jnp.where(row == col, both, 0.0), axis=0, keepdims=True)
    trace_in = jnp.sum(jnp.where(upper1, 0.0, diag), axis=1, keepdims=True)
    trace_out = jnp.sum(jnp.where(upper1, diag, 0.0), axis=1, keepdims=True)
    damp = 0.1 * jnp.where(upper1, trace_out, trace_in) / width
    both = both + jnp.where(row == col, damp, 0.0)
    inverse = negated_inverses(both, width)
    in_inv = inverse[:, :width]
    out_inv = jnp.where(upper, inverse, pltpu.roll(inverse, width, 1))

    q_load.wait()
    for s in range(seqs):
        sketch = grams[s][:width, width:]
        left = jnp.dot(in_inv, sketch, precision=HIGHEST, preferred_element_type=jnp.float32)
        precond = jnp.dot(left, out_inv, precision=HIGHEST, preferred_element_type=jnp.float32)
        precond = (precond * factor).astype(jnp.bfloat16).astype(jnp.float32)
        sums = [None] * 4
        for j in range(half):
            weights = jnp.where(upper1, precond[2 * j + 1 : 2 * j + 2, :], precond[2 * j : 2 * j + 1, :])
            term = q_v[:, 2 * width * j : 2 * width * (j + 1)].astype(jnp.float32) * weights
            sums[j % 4] = term if sums[j % 4] is None else sums[j % 4] + term
        acc = (sums[0] + sums[1]) + (sums[2] + sums[3])
        ones = jnp.ones((8, 2 * width), jnp.float32)
        scores = lax.dot_general(ones, acc, nt, precision=HIGHEST, preferred_element_type=jnp.float32)
        out_ref[s : s + 1, :] = scores[:1]

    for copy in a_copies:
        copy.wait_send()
    sent(0)
    repeat(1, n_dp, sent)


def solution(mesh):
    n_t, n_dp = mesh.shape["tensor"], mesh.shape["dp"]

    def shards(hidden_acts, out_grads, proj_in, proj_out, query_sketches):
        rows, depth = hidden_acts.shape
        model = out_grads.shape[1]
        width = proj_in.shape[1]
        queries, flat = query_sketches.shape
        seqs = n_dp // min(32, n_dp)
        share = rows // n_t
        groups = n_t // pair_of(n_t)
        dma = pltpu.SemaphoreType.DMA
        f32, bf16 = jnp.float32, jnp.bfloat16
        return pl.pallas_call(
            functools.partial(kernel, n_t, n_dp),
            out_shape=jax.ShapeDtypeStruct((seqs, queries), f32),
            in_specs=[pl.BlockSpec(memory_space=pltpu.HBM)] * 5,
            out_specs=pl.BlockSpec(memory_space=pltpu.VMEM),
            scratch_shapes=[
                pltpu.VMEM((rows, depth), bf16),
                pltpu.VMEM((rows, model), bf16),
                pltpu.VMEM((width, depth), bf16),
                pltpu.VMEM((width, model), bf16),
                pltpu.VMEM((queries, flat), bf16),
                pltpu.VMEM((rows, 2 * width), f32),
                pltpu.VMEM((n_t - 1, share, 2 * width), f32),
                pltpu.VMEM((n_dp * n_t, share, 2 * width), f32),
                dma((3,)),
                dma((2 * IN_CHUNKS,)),
                dma((n_t - 1,)),
                dma((n_t - 1,)),
                dma((n_dp, groups)),
                dma((n_dp, groups)),
                dma((n_dp, groups)),
                dma((n_dp, groups)),
            ],
            compiler_params=pltpu.CompilerParams(
                collective_id=0, has_side_effects=True
            ),
        )(hidden_acts, out_grads, proj_in.T, proj_out.T, query_sketches)

    return jax.shard_map(
        shards,
        mesh=mesh,
        in_specs=(
            P(("groups", "dp"), "tensor"),
            P(("groups", "dp"), "tensor"),
            P("tensor", None),
            P("tensor", None),
            P("dp", None),
        ),
        out_specs=P("groups", "dp"),
        check_vma=False,
    )
```

```python
import functools
import math

import jax
import jax.numpy as jnp
from jax import lax
from jax.experimental import pallas as pl
from jax.experimental.pallas import tpu as pltpu
from jax.sharding import PartitionSpec as P

MESH = pl.DeviceIdType.MESH
HIGHEST = lax.Precision.HIGHEST
IN_CHUNKS = 4
BLOCK = 8


def repeat(start, stop, body):
    if stop - start <= 8:
        for k in range(start, stop):
            body(k)
    else:
        lax.fori_loop(start, stop, lambda k, c: (body(k), c)[1], 0)


def pair_of(n_t):
    return 2 if n_t % 2 == 0 else 1


def negated_inverses(both, width):
    shape = both.shape
    row = lax.broadcasted_iota(jnp.int32, shape, 0)
    lane = lax.broadcasted_iota(jnp.int32, shape, 1)
    col = lane % width
    side = lane - col
    m = both
    for k0 in range(0, width, BLOCK):
        js = range(BLOCK)
        cols = [jnp.take_along_axis(m, side + (k0 + j), axis=1) for j in js]
        at = slice(k0, k0 + BLOCK)
        d = [cols[j][at, :] for j in js]
        unit = jnp.where(col[at] == row[at], -1.0, 0.0)
        w = jnp.where((col[at] >= k0) & (col[at] < k0 + BLOCK), unit, m[at, :])
        for p in js:
            pivot_row = row[at] == k0 + p
            f = d[p]
            r = 1.0 / f[p : p + 1, :]
            wp = w[p : p + 1, :] * r
            w = jnp.where(pivot_row, wp, w - f * wp)
            for j in range(p + 1, BLOCK):
                dp = d[j][p : p + 1, :] * r
                d[j] = jnp.where(pivot_row, dp, d[j] - f * dp)
        w = [w[j : j + 1, :] for j in js]
        in_rows = (row >= k0) & (row < k0 + BLOCK)
        in_cols = (col >= k0) & (col < k0 + BLOCK)
        m = jnp.where(in_rows | in_cols, 0.0, m)
        for j in js:
            c = jnp.where(in_rows, jnp.where(row == k0 + j, -1.0, 0.0), cols[j])
            m = m - c * w[j]
    return m


def kernel(
    n_t, n_dp, h_hbm, g_hbm, pi_hbm, po_hbm, q_hbm, out_ref,
    h_v, g_v, pi_v, po_v, q_v, part, landed, tokens,
    load_sem, h_sem, a_send, a_recv, b_send, b_recv, c_send, c_recv,
):
    me_t = lax.axis_index("tensor")
    me_dp = lax.axis_index("dp")
    pair = pair_of(n_t)
    width = pi_v.shape[0]
    rows = part.shape[0]
    share = rows // pair
    span = min(32, n_dp)
    seqs = n_dp // span
    token_count = rows * n_dp
    factor = 1.0 / math.sqrt(rows * span)

    barrier = pltpu.get_barrier_semaphore()

    def greet_t(k):
        pl.semaphore_signal(barrier, inc=1, device_id={"tensor": lax.rem(me_t + k, n_t)}, device_id_type=MESH)

    def greet_dp(k):
        pl.semaphore_signal(barrier, inc=1, device_id={"dp": lax.rem(me_dp + k, n_dp)}, device_id_type=MESH)

    repeat(1, n_t, greet_t)
    repeat(1, n_dp, greet_dp)

    step = h_v.shape[1] // IN_CHUNKS
    loads = [
        pltpu.make_async_copy(g_hbm, g_v, load_sem.at[0]),
        pltpu.make_async_copy(po_hbm, po_v, load_sem.at[1]),
    ]
    chunks = []
    for c in range(IN_CHUNKS):
        at = pl.ds(c * step, step)
        chunks.append(
            (
                pltpu.make_async_copy(h_hbm.at[:, at], h_v.at[:, at], h_sem.at[2 * c]),
                pltpu.make_async_copy(pi_hbm.at[:, at], pi_v.at[:, at], h_sem.at[2 * c + 1]),
            )
        )
    q_load = pltpu.make_async_copy(q_hbm, q_v, load_sem.at[2])
    for copy in loads:
        copy.start()
    for copies in chunks:
        for copy in copies:
            copy.start()
    q_load.start()

    nt = (((1,), (1,)), ((), ()))
    tn = (((0,), (0,)), ((), ()))
    for copy in loads:
        copy.wait()
    part[:, width:] = lax.dot_general(g_v[...], po_v[...], nt, preferred_element_type=jnp.float32)
    total = None
    for c, copies in enumerate(chunks):
        for copy in copies:
            copy.wait()
        at = pl.ds(c * step, step)
        term = lax.dot_general(h_v[:, at], pi_v[:, at], nt, preferred_element_type=jnp.float32)
        total = term if total is None else total + term
    part[:, :width] = total

    pl.semaphore_wait(barrier, (n_t - 1) + (n_dp - 1))

    def share_of(t):
        return pl.ds(pl.multiple_of(lax.rem(t, pair) * share, share), share)

    def a_copy(k, slot):
        peer = lax.rem(me_t + k, n_t)
        return pltpu.make_async_remote_copy(
            src_ref=part.at[share_of(peer)],
            dst_ref=landed.at[slot],
            send_sem=a_send.at[k - 1],
            recv_sem=a_recv.at[k - 1],
            device_id={"tensor": peer},
            device_id_type=MESH,
        )

    for k in range(1, n_t):
        a_copy(k, me_t).start()
    landed[me_t] = part[share_of(me_t), :]
    for k in range(1, n_t):
        a_copy(k, lax.rem(me_t + n_t - k, n_t)).wait_recv()
    mine = landed[0]
    for t in range(1, n_t):
        mine = mine + landed[t]
    side = lax.rem(me_t, pair)
    tokens[me_dp * pair + side] = mine

    def b_copy(k, dp):
        slot = dp * pair + side
        return pltpu.make_async_remote_copy(
            src_ref=tokens.at[slot],
            dst_ref=tokens.at[slot],
            send_sem=b_send.at[k],
            recv_sem=b_recv.at[k],
            device_id={"dp": lax.rem(me_dp + k, n_dp)},
            device_id_type=MESH,
        )

    def c_copy(k, at_side):
        slot = lax.rem(me_dp + n_dp - k, n_dp) * pair + at_side
        return pltpu.make_async_remote_copy(
            src_ref=tokens.at[slot],
            dst_ref=tokens.at[slot],
            send_sem=c_send.at[k],
            recv_sem=c_recv.at[k],
            device_id={"tensor": me_t + 1 - 2 * side},
            device_id_type=MESH,
        )

    def take(k):
        b_copy(k, lax.rem(me_dp + n_dp - k, n_dp)).wait_recv()
        if pair == 2:
            c_copy(k, side).start()

    repeat(1, n_dp, lambda k: b_copy(k, me_dp).start())
    if pair == 2:
        c_copy(0, side).start()
    repeat(1, n_dp, take)
    if pair == 2:
        c_copy(0, 1 - side).wait_recv()
        repeat(1, n_dp, lambda k: c_copy(k, 1 - side).wait_recv())

    upper = lax.broadcasted_iota(jnp.int32, (width, 2 * width), 1) >= width
    upper1 = lax.broadcasted_iota(jnp.int32, (1, 2 * width), 1) >= width
    half = width // 2
    both = None
    grams = []
    for s in range(seqs):
        own = tokens[s * span * pair : (s + 1) * span * pair].reshape(span * rows, 2 * width)
        gram = lax.dot_general(own, own, tn, precision=HIGHEST, preferred_element_type=jnp.float32)
        cov = jnp.where(upper, gram[width:], gram[:width])
        both = cov if both is None else both + cov
        grams.append(gram)
    both = both / token_count
    row = lax.broadcasted_iota(jnp.int32, both.shape, 0)
    col = lax.broadcasted_iota(jnp.int32, both.shape, 1) % width
    diag = jnp.sum(jnp.where(row == col, both, 0.0), axis=0, keepdims=True)
    trace_in = jnp.sum(jnp.where(upper1, 0.0, diag), axis=1, keepdims=True)
    trace_out = jnp.sum(jnp.where(upper1, diag, 0.0), axis=1, keepdims=True)
    damp = 0.1 * jnp.where(upper1, trace_out, trace_in) / width
    both = both + jnp.where(row == col, damp, 0.0)
    inverse = negated_inverses(both, width)
    in_inv = inverse[:, :width]
    out_inv = jnp.where(upper, inverse, pltpu.roll(inverse, width, 1))

    q_load.wait()
    for s in range(seqs):
        sketch = grams[s][:width, width:]
        left = jnp.dot(in_inv, sketch, precision=HIGHEST, preferred_element_type=jnp.float32)
        precond = jnp.dot(left, out_inv, precision=HIGHEST, preferred_element_type=jnp.float32)
        precond = (precond * factor).astype(jnp.bfloat16).astype(jnp.float32)
        sums = [None] * 4
        for j in range(half):
            weights = jnp.where(upper1, precond[2 * j + 1 : 2 * j + 2, :], precond[2 * j : 2 * j + 1, :])
            term = q_v[:, 2 * width * j : 2 * width * (j + 1)].astype(jnp.float32) * weights
            sums[j % 4] = term if sums[j % 4] is None else sums[j % 4] + term
        acc = (sums[0] + sums[1]) + (sums[2] + sums[3])
        ones = jnp.ones((8, 2 * width), jnp.float32)
        scores = lax.dot_general(ones, acc, nt, precision=HIGHEST, preferred_element_type=jnp.float32)
        out_ref[s : s + 1, :] = scores[:1]

    for k in range(1, n_t):
        a_copy(k, me_t).wait_send()
    repeat(1, n_dp, lambda k: b_copy(k, me_dp).wait_send())
    if pair == 2:
        c_copy(0, side).wait_send()
        repeat(1, n_dp, lambda k: c_copy(k, side).wait_send())


def solution(mesh):
    n_t, n_dp = mesh.shape["tensor"], mesh.shape["dp"]

    def shards(hidden_acts, out_grads, proj_in, proj_out, query_sketches):
        rows, depth = hidden_acts.shape
        model = out_grads.shape[1]
        width = proj_in.shape[1]
        queries, flat = query_sketches.shape
        seqs = n_dp // min(32, n_dp)
        pair = pair_of(n_t)
        share = rows // pair
        dma = pltpu.SemaphoreType.DMA
        f32, bf16 = jnp.float32, jnp.bfloat16
        return pl.pallas_call(
            functools.partial(kernel, n_t, n_dp),
            out_shape=jax.ShapeDtypeStruct((seqs, queries), f32),
            in_specs=[pl.BlockSpec(memory_space=pltpu.HBM)] * 5,
            out_specs=pl.BlockSpec(memory_space=pltpu.VMEM),
            scratch_shapes=[
                pltpu.VMEM((rows, depth), bf16),
                pltpu.VMEM((rows, model), bf16),
                pltpu.VMEM((width, depth), bf16),
                pltpu.VMEM((width, model), bf16),
                pltpu.VMEM((queries, flat), bf16),
                pltpu.VMEM((rows, 2 * width), f32),
                pltpu.VMEM((n_t, share, 2 * width), f32),
                pltpu.VMEM((n_dp * pair, share, 2 * width), f32),
                dma((3,)),
                dma((2 * IN_CHUNKS,)),
                dma((n_t - 1,)),
                dma((n_t - 1,)),
                dma((n_dp,)),
                dma((n_dp,)),
                dma((n_dp,)),
                dma((n_dp,)),
            ],
            compiler_params=pltpu.CompilerParams(
                collective_id=0, has_side_effects=True
            ),
        )(hidden_acts, out_grads, proj_in.T, proj_out.T, query_sketches)

    return jax.shard_map(
        shards,
        mesh=mesh,
        in_specs=(
            P(("groups", "dp"), "tensor"),
            P(("groups", "dp"), "tensor"),
            P("tensor", None),
            P("tensor", None),
            P("dp", None),
        ),
        out_specs=P("groups", "dp"),
        check_vma=False,
    )
```
